32 devices in a mesh: groups: 2 (over y), pool: 4 (over z), tp: 4 (over x, core).
Axes of the slice: x: 2, y: 2, z: 4, core: 2. Of those that a mesh axis runs over, the one named last changes fastest.
Arguments:
- tokens: bfloat16 [2560, 8192], P(('groups', 'pool'), 'tp'), parts along dimension 0, may hold values from -6 to 6
- w_kv: bfloat16 [8192, 8, 256], P('tp'), may hold values from -0.0625 to 0.0625
- prompt_lens: int32 [32], P('groups'), parts along dimension 0, may hold values from 1 to 640, 1280 in all
- routes: int32 [320, 1], P('groups'), parts along dimension 0, may hold values from 0 to 3; in each aligned block of 40 rows (0 to 39, 40 to 79, ...) at most 20 rows name the same one
Outputs:
- handed: bfloat16 [8, 4, 20, 8, 8, 256], P(('groups', 'pool'), None, None, None, 'tp'), parts along dimension 0
The draws below stay inside these ranges and needn't reach their ends.
There are 2 independent parts, one for each index of `groups`. The reference program is written for one: setup_inputs(seed, part) draws one part's arguments, and reference() takes and returns one part's arrays. A program takes and returns all parts, laid end to end along the dimension named above; an argument that names none is the same for every part. Nothing has to cross between parts.
Inputs may be any that keep to these rules, and one draw needn't show every extreme that they name: `routes`: each pool index's 40 pages name every destination at most 20 times.
All inputs are finite; a program needn't handle non-finite values.
Results may differ from the reference program's by a relative error of at most 0.001.
Values may be sent and summed in bfloat16 or wider, within the bound.
A program may use at most 64 MiB of HBM per device.

```python
import math
import jax
import jax.numpy as jnp
import numpy as np

D = 8192
KV_HEADS = 8
HEAD_DIM = 128
PRE_TOK = 320
BLOCK = 8
TOKENS = 1280
PROMPTS = 16
P_DEV = 40
PAGES = 160
MOST = 20
N_POOL = 4


def level_of(stream_key, extent, shards, least, top_value):
    def one(position, blocks):
        draws = jax.random.uniform(jax.random.fold_in(jax.random.fold_in(stream_key, 6), position), (blocks,), jnp.float32, least / len(shards), top_value / len(shards))
        return jnp.repeat(jnp.exp(draws), extent[position] // blocks).reshape((-1,) + (1,) * (len(extent) - position - 1))

    loudness = one(*shards[0])
    for cut in shards[1:]:
        loudness = loudness * one(*cut)
    return loudness


def length_profile(number_of, total, reach, slope):
    portions = [(1 << 20) // math.isqrt(grade ** slope) + 1 for grade in range(2, number_of + 1)]
    surplus, holding = total - reach - (number_of - 1), [1] * (number_of - 1)
    while surplus > 0:
        movable = [i for i in range(number_of - 1) if holding[i] < reach]
        whole, budget = sum([portions[i] for i in movable]), surplus
        for i in movable:
            addition = min(reach - holding[i], max(1, budget * portions[i] // whole), surplus)
            holding[i] = holding[i] + addition
            surplus = surplus - addition
    return np.array([reach] + holding)


def uneven(own_key, count, total, bound, lean):
    if count == 2:
        one = jax.random.randint(own_key, (), max(1, total - bound), min(bound, total - 1) + 1)
        return jnp.stack([one, total - one])
    tallies = jnp.asarray(length_profile(count, total, bound, lean), jnp.int32)
    couples = (count - 1) // 2
    source_of, sink = tallies[1:1 + 2 * couples:2], tallies[2:2 + 2 * couples:2]
    margin = jnp.minimum(source_of - 1, bound - sink)
    passed = jax.random.randint(jax.random.fold_in(own_key, 1), (couples,), 0, 1 << 20) % (margin + 1)
    tallies = tallies.at[1:1 + 2 * couples:2].set(source_of - passed).at[2:2 + 2 * couples:2].set(sink + passed)
    return tallies[jax.random.permutation(jax.random.fold_in(own_key, 2), count)]


def shared_out(own_key, own, number, rows, amount, top, reach, skew):
    sequence = jax.random.permutation(own_key, amount)
    packed, usual = shares(amount, rows * top, reach, skew, True), shares(amount, rows * top, reach, skew, False)
    places = jnp.arange(amount)

    def named(sizes, rotation):
        used = int((sizes > 0).sum())
        fixed = max(1, used // 4)
        shifted = fixed + (places - fixed + rotation * (used - fixed)) % max(1, amount - fixed)
        return jnp.zeros((amount,), jnp.int32).at[sequence[jnp.where(places < fixed, places, shifted)]].set(jnp.asarray(sizes, jnp.int32))

    sizes = jnp.where(number % 4 == 0, named(packed, number // 4), named(usual, number - number // 4 - 1))
    mixed = jax.random.permutation(jax.random.fold_in(own, 3), amount)
    donor, taker = mixed[0:amount // 2 * 2:2], mixed[1:amount // 2 * 2:2]
    slack = jnp.minimum(sizes[donor] - 1, reach - sizes[taker]) // 2
    slack = jnp.where((donor == sequence[0]) | (taker == sequence[0]) | (sizes[taker] == 0), 0, jnp.maximum(slack, 0))
    shifted = jax.random.randint(jax.random.fold_in(own, 4), (amount // 2,), 0, 1 << 20) % (slack + 1)
    sizes = sizes.at[donor].add(-shifted).at[taker].add(shifted)
    items = jnp.searchsorted(jnp.cumsum(sizes), jnp.arange(rows * top), side="right").astype(jnp.int32)
    listing = items.reshape(top, rows).T
    listing = listing[jax.random.permutation(jax.random.fold_in(own, 1), rows)]
    rotation = jax.random.randint(jax.random.fold_in(own, 2), (rows, 1), 0, top)
    return jnp.take_along_axis(listing, (jnp.arange(top)[None, :] + rotation) % top, axis=1)


def shares(number_of, total, most, slope, full):
    weights = [(1 << 20) // math.isqrt(standing ** slope) + 1 for standing in range(1, number_of + 1)]
    largest = most if full else min(most, max(-(-total // number_of), total * weights[0] // sum(weights)))
    least = 1 if total - largest >= number_of - 1 else 0
    holding, surplus = [largest] + [least] * (number_of - 1), total - largest - least * (number_of - 1)
    while surplus > 0:
        movable = [i for i in range(1, number_of) if holding[i] < largest] or [i for i in range(1, number_of) if holding[i] < most]
        whole, budget = sum([weights[i] for i in movable]), surplus
        for i in movable:
            more = min(most - holding[i], max(1, budget * weights[i] // whole), surplus)
            holding[i] = holding[i] + more
            surplus = surplus - more
    return np.array(holding)


def bell_draw(rng, extent, spread, limit, split=(), kind=jnp.bfloat16):
    loudness = level_of(rng, extent, split, -0.22, 0.18) if split else 1.0
    drawn = jax.random.normal(rng, extent, jnp.float32) * spread * loudness
    return jnp.minimum(jnp.maximum(drawn, -limit), limit).astype(kind)


def setup_inputs(seed: int = 0, part: int = 0) -> dict:
    splits = jax.random.split(jax.random.key(seed), 5)
    part_keys = jax.random.split(jax.random.fold_in(splits[4], part), 5)
    tokens = bell_draw(part_keys[0], (TOKENS, D), 1.0, 6.0, ((0, 4), (1, 4)))
    w_kv = bell_draw(splits[1], (D, KV_HEADS, 2 * HEAD_DIM), D ** -0.5, 0.0625, ((0, 4),))
    prompt_lens = uneven(part_keys[2], PROMPTS, TOKENS, 2 * PRE_TOK, 2).astype(jnp.int32)
    routes_keys = jax.random.split(jax.random.fold_in(part_keys[3], 1), PAGES // P_DEV)
    routes_turns = jax.random.permutation(jax.random.fold_in(part_keys[3], 3), PAGES // P_DEV)
    routes = jax.vmap(lambda own, number: shared_out(jax.random.fold_in(part_keys[3], 2), own, number, P_DEV, N_POOL, 1, MOST, 2))(routes_keys, routes_turns).reshape((PAGES, 1))
    return {"tokens": tokens, "w_kv": w_kv, "prompt_lens": prompt_lens, "routes": routes}


def frequencies(head_dim):
    half = head_dim // 2
    base = jnp.exp(jnp.arange(half, dtype=jnp.float32) * (-2.0 / head_dim) * jnp.log(jnp.float32(500000.0)))
    wavelength = (2.0 * math.pi) / base
    smooth = (8192.0 / wavelength - 1.0) / 3.0
    middle = (1.0 - smooth) * base / 8.0 + smooth * base
    return jnp.where(wavelength < 2048.0, base, jnp.where(wavelength > 8192.0, base / 8.0, middle))


def rotate(key_rows, positions):
    half = key_rows.shape[-1] // 2
    freqs = frequencies(key_rows.shape[-1])
    angle = positions.astype(jnp.float32)[:, None] * freqs[None, :]
    cosine = jnp.cos(angle)[:, None, :]
    sine = jnp.sin(angle)[:, None, :]
    first = key_rows[..., :half]
    second = key_rows[..., half:]
    return jnp.concatenate([first * cosine - second * sine, second * cosine + first * sine], axis=-1)


def offsets(token_index, prompt_lens):
    prompt_ends = jnp.cumsum(prompt_lens).astype(jnp.int32)
    before = jnp.sum(jnp.where(prompt_ends[None, :] <= token_index[:, None], prompt_lens[None, :], 0), axis=1)
    return (token_index - before).astype(jnp.int32)


def reference(tokens, w_kv, prompt_lens, routes):
    kv_rows = jnp.dot(tokens, w_kv.reshape(D, KV_HEADS * 2 * HEAD_DIM), preferred_element_type=jnp.float32)
    kv_rows = kv_rows.reshape(TOKENS, KV_HEADS, 2 * HEAD_DIM)
    positions = offsets(jnp.arange(TOKENS, dtype=jnp.int32), prompt_lens)
    rotated = rotate(kv_rows[..., :HEAD_DIM], positions)
    pages = jnp.concatenate([rotated, kv_rows[..., HEAD_DIM:]], axis=-1).astype(jnp.bfloat16)
    pages = pages.reshape(PAGES, BLOCK, KV_HEADS, 2 * HEAD_DIM)
    targets = routes[:, 0].reshape(N_POOL, P_DEV)
    matches = (targets[:, :, None] == jnp.arange(N_POOL, dtype=jnp.int32)[None, None, :]).astype(jnp.int32)
    ranking = jnp.sum((jnp.cumsum(matches, axis=1) - matches) * matches, axis=2).reshape(PAGES).astype(jnp.int32)
    sources = (jnp.arange(PAGES, dtype=jnp.int32) // P_DEV).astype(jnp.int32)
    handed = jnp.zeros((N_POOL, N_POOL, MOST, BLOCK, KV_HEADS, 2 * HEAD_DIM), jnp.bfloat16)
    handed = handed.at[routes[:, 0], sources, ranking].set(pages)
    return handed
```

```python
import functools
import math

import jax
import jax.numpy as jnp
from jax import lax
from jax.experimental import pallas as pl
from jax.experimental.pallas import tpu as pltpu
from jax.sharding import PartitionSpec as P

BLOCK = 8
LANES = 128
MESH = pl.DeviceIdType.MESH


def frequencies(head_dim):
    half = head_dim // 2
    base = jnp.exp(
        jnp.arange(half, dtype=jnp.float32) * (-2.0 / head_dim) * jnp.log(jnp.float32(500000.0))
    )
    wavelength = 2.0 * math.pi / base
    smooth = (8192.0 / wavelength - 1.0) / 3.0
    middle = (1.0 - smooth) * base / 8.0 + smooth * base
    return jnp.where(wavelength < 2048.0, base, jnp.where(wavelength > 8192.0, base / 8.0, middle))


def hand_over(
    pool_size, tp_size, most,
    partial_ref, freq_ref, lens_row_ref, lens_col_ref, route_row_ref, route_col_ref,
    out_ref,
    pair_in, across_out, across_in, placed, select, cosine, sine,
    pair_sems, across_sems, pool_sems, local_sems,
):
    pool_index = lax.axis_index("pool")
    tp_index = lax.axis_index("tp")
    chip, core = tp_index // 2, tp_index % 2
    chips = tp_size // 2
    rows = partial_ref.shape[1]
    local_heads = partial_ref.shape[0] // tp_size
    parts = partial_ref.shape[2] // LANES
    chunks = [(j, part) for j in range(local_heads) for part in range(parts)]
    span = most * BLOCK
    page_count = rows // BLOCK
    slot_rows = pool_size * span

    def head_of(chip_of, core_of, j):
        return (chip_of * 2 + core_of) * local_heads + j

    barrier = pltpu.get_barrier_semaphore()
    peers = [{"tp": chip * 2 + 1 - core}]
    peers += [{"tp": lax.rem(chip + d, chips) * 2 + core} for d in range(1, chips)]
    peers += [{"pool": lax.rem(pool_index + d, pool_size)} for d in range(1, pool_size)]
    for peer in peers:
        pl.semaphore_signal(barrier, inc=1, device_id=peer, device_id_type=MESH)
    pl.semaphore_wait(barrier, len(peers))

    def window(head, part):
        return partial_ref.at[head, :, pl.ds(part * LANES, LANES)]

    def pair_copy(n, d):
        j, part = chunks[n]
        return pltpu.make_async_remote_copy(
            src_ref=window(head_of(lax.rem(chip + d, chips), 1 - core, j), part),
            dst_ref=pair_in.at[n, d],
            send_sem=pair_sems.at[0, n, d],
            recv_sem=pair_sems.at[1, n, d],
            device_id={"tp": chip * 2 + 1 - core},
            device_id_type=MESH,
        )

    def across_copy(n, d):
        return pltpu.make_async_remote_copy(
            src_ref=across_out.at[n, d - 1],
            dst_ref=across_in.at[n, d - 1],
            send_sem=across_sems.at[0, n, d - 1],
            recv_sem=across_sems.at[1, n, d - 1],
            device_id={"tp": lax.rem(chip + d, chips) * 2 + core},
            device_id_type=MESH,
        )

    def pool_copy(n, d):
        target = lax.rem(pool_index + d, pool_size)
        return pltpu.make_async_remote_copy(
            src_ref=placed.at[n, pl.ds(pl.multiple_of(target * span, span), span)],
            dst_ref=out_ref.at[
                pl.ds(pl.multiple_of(pool_index * span, span), span), pl.ds(n * LANES, LANES)
            ],
            send_sem=pool_sems.at[0, n, d - 1],
            recv_sem=pool_sems.at[1, n, d - 1],
            device_id={"pool": target},
            device_id_type=MESH,
        )

    def own_copy(n):
        block = pl.ds(pl.multiple_of(pool_index * span, span), span)
        return pltpu.make_async_copy(
            placed.at[n, block], out_ref.at[block, pl.ds(n * LANES, LANES)], local_sems.at[n]
        )

    hops = [d % chips for d in range(1, chips + 1)]
    for n in range(len(chunks)):
        for d in hops:
            pair_copy(n, d).start()
    for n, (j, part) in enumerate(chunks):
        for d in range(1, chips):
            pair_copy(n, d).wait_recv()
            head = head_of(lax.rem(chip + d, chips), core, j)
            across_out[n, d - 1] = (
                partial_ref[head, :, part * LANES:(part + 1) * LANES] + pair_in[n, d]
            )
            across_copy(n, d).start()

    def iota(shape, axis):
        return lax.broadcasted_iota(jnp.int32, shape, axis)

    prompts = lens_row_ref.shape[1]
    upto = iota((prompts, prompts), 0) <= iota((prompts, prompts), 1)
    ends = jnp.sum(jnp.where(upto, lens_col_ref[...].astype(jnp.float32), 0.0), axis=0, keepdims=True)
    token = (pool_index * rows + iota((rows, prompts), 0)).astype(jnp.float32)
    before = jnp.sum(
        jnp.where(ends <= token, lens_row_ref[...].astype(jnp.float32), 0.0), axis=1, keepdims=True
    )
    position = token[:, :1] - before
    angle = position * freq_ref[...]
    cosine[...] = jnp.cos(angle)
    turned = jnp.sin(angle)
    sine[...] = jnp.where(iota((rows, LANES), 1) < LANES // 2, -turned, turned)

    pages = route_row_ref.shape[1]
    first = pool_index * page_count
    target_row = jnp.sum(
        jnp.where(
            iota((pages, rows), 0) == first + (iota((pages, rows), 1) >> 3),
            route_col_ref[...].astype(jnp.float32),
            0.0,
        ),
        axis=0,
        keepdims=True,
    )
    target_col = jnp.sum(
        jnp.where(
            iota((rows, pages), 1) == first + (iota((rows, pages), 0) >> 3),
            route_row_ref[...].astype(jnp.float32),
            0.0,
        ),
        axis=1,
        keepdims=True,
    )
    earlier = (iota((rows, rows), 0) >> 3) < (iota((rows, rows), 1) >> 3)
    rank = jnp.sum(
        jnp.where(earlier & (target_col == target_row), 1.0, 0.0), axis=0, keepdims=True
    )
    slot = target_row * span + rank + (iota((1, rows), 1) & 7).astype(jnp.float32)
    select[...] = jnp.where(
        iota((slot_rows, rows), 0).astype(jnp.float32) == slot, 1.0, 0.0
    ).astype(jnp.bfloat16)

    for n, (j, part) in enumerate(chunks):
        pair_copy(n, 0).wait_recv()
        total = (
            partial_ref[head_of(chip, core, j), :, part * LANES:(part + 1) * LANES] + pair_in[n, 0]
        )
        for d in range(1, chips):
            across_copy(n, d).wait_recv()
            total = total + across_in[n, d - 1]
        if part == 0:
            half = LANES // 2
            swapped = jnp.concatenate([total[:, half:], total[:, :half]], axis=1)
            total = total * cosine[...] + swapped * sine[...]
        placed[n] = jnp.dot(
            select[...], total.astype(jnp.bfloat16), preferred_element_type=jnp.float32
        ).astype(jnp.bfloat16)
        for d in range(1, pool_size):
            pool_copy(n, d).start()
        own_copy(n).start()

    for n in range(len(chunks)):
        own_copy(n).wait()
        for d in range(chips):
            pair_copy(n, d).wait_send()
        for d in range(1, chips):
            across_copy(n, d).wait_send()
        for d in range(1, pool_size):
            pool_copy(n, d).wait()


def on_device(pool_size, tp_size, tokens, w_kv, prompt_lens, routes):
    rows = tokens.shape[0]
    heads, width = w_kv.shape[1:]
    local_heads = heads // tp_size
    most = max(2, 2 * (rows // BLOCK) // pool_size)
    slot_rows = pool_size * most * BLOCK
    partial = jnp.einsum("td,dkc->ktc", tokens, w_kv, preferred_element_type=jnp.float32)
    freqs = frequencies(width // 2)
    chunks = local_heads * width // LANES
    chips = tp_size // 2
    vmem = pl.BlockSpec(memory_space=pltpu.VMEM)
    received = pl.pallas_call(
        functools.partial(hand_over, pool_size, tp_size, most),
        out_shape=jax.ShapeDtypeStruct((slot_rows, local_heads * width), jnp.bfloat16),
        in_specs=[vmem] * 6,
        out_specs=vmem,
        scratch_shapes=[
            pltpu.VMEM((chunks, chips, rows, LANES), jnp.float32),
            pltpu.VMEM((chunks, chips - 1, rows, LANES), jnp.float32),
            pltpu.VMEM((chunks, chips - 1, rows, LANES), jnp.float32),
            pltpu.VMEM((chunks, slot_rows, LANES), jnp.bfloat16),
            pltpu.VMEM((slot_rows, rows), jnp.bfloat16),
            pltpu.VMEM((rows, LANES), jnp.float32),
            pltpu.VMEM((rows, LANES), jnp.float32),
            pltpu.SemaphoreType.DMA((2, chunks, chips)),
            pltpu.SemaphoreType.DMA((2, chunks, chips - 1)),
            pltpu.SemaphoreType.DMA((2, chunks, pool_size - 1)),
            pltpu.SemaphoreType.DMA((chunks,)),
        ],
        compiler_params=pltpu.CompilerParams(
            collective_id=0, has_side_effects=True, vmem_limit_bytes=40 * 2**20
        ),
    )(
        partial,
        jnp.concatenate([freqs, freqs])[None, :],
        prompt_lens[None, :],
        prompt_lens[:, None],
        routes.reshape(1, -1),
        routes,
    )
    return received.reshape(1, pool_size, most, BLOCK, local_heads, width)


def solution(mesh):
    placed = (P(("groups", "pool"), "tp"), P("tp", None, None), P("groups"), P("groups", None))
    return jax.shard_map(
        functools.partial(on_device, mesh.shape["pool"], mesh.shape["tp"]),
        mesh=mesh,
        in_specs=placed,
        out_specs=P(("groups", "pool"), None, None, None, "tp", None),
        check_vma=False,
    )
```

```python
import functools
import math

import jax
import jax.numpy as jnp
from jax import lax
from jax.experimental import pallas as pl
from jax.experimental.pallas import tpu as pltpu
from jax.sharding import PartitionSpec as P

BLOCK = 8
LANES = 128
DEPTH = 256
MESH = pl.DeviceIdType.MESH


def frequencies(head_dim):
    half = head_dim // 2
    base = jnp.exp(
        jnp.arange(half, dtype=jnp.float32) * (-2.0 / head_dim) * jnp.log(jnp.float32(500000.0))
    )
    wavelength = 2.0 * math.pi / base
    smooth = (8192.0 / wavelength - 1.0) / 3.0
    middle = (1.0 - smooth) * base / 8.0 + smooth * base
    return jnp.where(wavelength < 2048.0, base, jnp.where(wavelength > 8192.0, base / 8.0, middle))


def hand_over(
    pool_size, tp_size, most,
    tokens_hbm, w_hbm, freq_ref, lens_ref, route_ref,
    out_ref,
    tokens, w_in, w_heads, partial,
    pair_in, across_out, across_in, placed, select, cosine, sine,
    in_sems, pair_sems, across_sems, pool_sems, local_sems,
):
    pool_index = lax.axis_index("pool")
    tp_index = lax.axis_index("tp")
    chip, core = tp_index // 2, tp_index % 2
    chips = tp_size // 2
    rows = tokens.shape[0]
    local_heads = partial.shape[0] // tp_size
    parts = partial.shape[2] // LANES
    chunks = [(j, part) for j in range(local_heads) for part in range(parts)]
    span = most * BLOCK
    page_count = rows // BLOCK
    slot_rows = pool_size * span

    tokens_in = pltpu.make_async_copy(tokens_hbm, tokens, in_sems.at[0])
    depth = min(DEPTH, w_in.shape[0])
    steps = w_in.shape[0] // depth
    w_copies = [
        pltpu.make_async_copy(
            w_hbm.at[pl.ds(i * depth, depth)], w_in.at[pl.ds(i * depth, depth)], in_sems.at[i + 1]
        )
        for i in range(steps)
    ]
    for copy in w_copies:
        copy.start()
    tokens_in.start()

    def head_of(chip_of, core_of, j):
        return (chip_of * 2 + core_of) * local_heads + j

    barrier = pltpu.get_barrier_semaphore()
    peers = [{"tp": chip * 2 + 1 - core}]
    peers += [{"tp": lax.rem(chip + d, chips) * 2 + core} for d in range(1, chips)]
    peers += [{"pool": lax.rem(pool_index + d, pool_size)} for d in range(1, pool_size)]
    for peer in peers:
        pl.semaphore_signal(barrier, inc=1, device_id=peer, device_id_type=MESH)

    for i, copy in enumerate(w_copies):
        copy.wait()
        block = slice(i * depth, (i + 1) * depth)
        w_heads[:, block, :] = jnp.swapaxes(w_in[block], 0, 1)
    tokens_in.wait()

    def multiply(head):
        partial[head] = jnp.dot(tokens[...], w_heads[head], preferred_element_type=jnp.float32)

    def window(head, part):
        return partial.at[head, :, pl.ds(part * LANES, LANES)]

    def pair_copy(n, d):
        j, part = chunks[n]
        return pltpu.make_async_remote_copy(
            src_ref=window(head_of(lax.rem(chip + d, chips), 1 - core, j), part),
            dst_ref=pair_in.at[n, d],
            send_sem=pair_sems.at[0, n, d],
            recv_sem=pair_sems.at[1, n, d],
            device_id={"tp": chip * 2 + 1 - core},
            device_id_type=MESH,
        )

    def across_copy(n, d):
        return pltpu.make_async_remote_copy(
            src_ref=across_out.at[n, d - 1],
            dst_ref=across_in.at[n, d - 1],
            send_sem=across_sems.at[0, n, d - 1],
            recv_sem=across_sems.at[1, n, d - 1],
            device_id={"tp": lax.rem(chip + d, chips) * 2 + core},
            device_id_type=MESH,
        )

    def pool_copy(n, d):
        target = lax.rem(pool_index + d, pool_size)
        return pltpu.make_async_remote_copy(
            src_ref=placed.at[n, pl.ds(pl.multiple_of(target * span, span), span)],
            dst_ref=out_ref.at[
                pl.ds(pl.multiple_of(pool_index * span, span), span), pl.ds(n * LANES, LANES)
            ],
            send_sem=pool_sems.at[0, n, d - 1],
            recv_sem=pool_sems.at[1, n, d - 1],
            device_id={"pool": target},
            device_id_type=MESH,
        )

    def own_copy(n):
        block = pl.ds(pl.multiple_of(pool_index * span, span), span)
        return pltpu.make_async_copy(
            placed.at[n, block], out_ref.at[block, pl.ds(n * LANES, LANES)], local_sems.at[n]
        )

    def to_pair(j, d):
        multiply(head_of(lax.rem(chip + d, chips), 1 - core, j))
        for part in range(parts):
            pair_copy(j * parts + part, d).start()

    def to_others(j, d):
        for part in range(parts):
            n = j * parts + part
            pair_copy(n, d).wait_recv()
            head = head_of(lax.rem(chip + d, chips), core, j)
            across_out[n, d - 1] = (
                partial[head, :, part * LANES:(part + 1) * LANES] + pair_in[n, d]
            )
            across_copy(n, d).start()

    pl.semaphore_wait(barrier, len(peers))
    others = [(j, d) for j in range(local_heads) for d in range(1, chips)]
    to_pair(*others[0])
    multiply(head_of(lax.rem(chip + others[0][1], chips), core, others[0][0]))
    for j, d in others[1:]:
        to_pair(j, d)
    for j in range(local_heads):
        to_pair(j, 0)
    to_others(*others[0])
    for j, d in others[1:]:
        multiply(head_of(lax.rem(chip + d, chips), core, j))
        to_others(j, d)
    for j in range(local_heads):
        multiply(head_of(chip, core, j))

    def iota(shape, axis):
        return lax.broadcasted_iota(jnp.int32, shape, axis)

    def turned_row(column):
        count = column.shape[0]
        same = iota((count, count), 0) == iota((count, count), 1)
        return jnp.sum(jnp.where(same, column, 0.0), axis=0, keepdims=True)

    prompts = lens_ref.shape[1]
    lens = lens_ref[...].astype(jnp.float32)
    upto = iota((prompts, prompts), 1) <= iota((prompts, prompts), 0)
    ends = turned_row(jnp.sum(jnp.where(upto, lens, 0.0), axis=1, keepdims=True))
    token = (pool_index * rows + iota((rows, prompts), 0)).astype(jnp.float32)
    before = jnp.sum(jnp.where(ends <= token, lens, 0.0), axis=1, keepdims=True)
    position = token[:, :1] - before
    angle = position * freq_ref[...]
    cosine[...] = jnp.cos(angle)
    turned = jnp.sin(angle)
    sine[...] = jnp.where(iota((rows, LANES), 1) < LANES // 2, -turned, turned)

    pages = route_ref.shape[1]
    own_page = pool_index * page_count + (iota((rows, pages), 0) >> 3)
    target_col = jnp.sum(
        jnp.where(iota((rows, pages), 1) == own_page, route_ref[...].astype(jnp.float32), 0.0),
        axis=1,
        keepdims=True,
    )
    target_row = turned_row(target_col)
    earlier = (iota((rows, rows), 0) >> 3) < (iota((rows, rows), 1) >> 3)
    rank = jnp.sum(
        jnp.where(earlier & (target_col == target_row), 1.0, 0.0), axis=0, keepdims=True
    )
    slot = target_row * span + rank + (iota((1, rows), 1) & 7).astype(jnp.float32)
    select[...] = jnp.where(
        iota((slot_rows, rows), 0).astype(jnp.float32) == slot, 1.0, 0.0
    ).astype(jnp.bfloat16)

    for n, (j, part) in enumerate(chunks):
        pair_copy(n, 0).wait_recv()
        total = partial[head_of(chip, core, j), :, part * LANES:(part + 1) * LANES] + pair_in[n, 0]
        for d in range(1, chips):
            across_copy(n, d).wait_recv()
            total = total + across_in[n, d - 1]
        if part == 0:
            half = LANES // 2
            swapped = jnp.concatenate([total[:, half:], total[:, :half]], axis=1)
            total = total * cosine[...] + swapped * sine[...]
        placed[n] = jnp.dot(
            select[...], total.astype(jnp.bfloat16), preferred_element_type=jnp.float32
        ).astype(jnp.bfloat16)
        for d in range(1, pool_size):
            pool_copy(n, d).start()
        own_copy(n).start()

    for n in range(len(chunks)):
        own_copy(n).wait()
        for d in range(chips):
            pair_copy(n, d).wait_send()
        for d in range(1, chips):
            across_copy(n, d).wait_send()
        for d in range(1, pool_size):
            pool_copy(n, d).wait()


def on_device(pool_size, tp_size, tokens, w_kv, prompt_lens, routes):
    rows = tokens.shape[0]
    features, heads, width = w_kv.shape
    local_heads = heads // tp_size
    most = max(2, 2 * (rows // BLOCK) // pool_size)
    slot_rows = pool_size * most * BLOCK
    freqs = frequencies(width // 2)
    chunks = local_heads * width // LANES
    chips = tp_size // 2
    steps = max(1, features // DEPTH)
    vmem = pl.BlockSpec(memory_space=pltpu.VMEM)
    hbm = pl.BlockSpec(memory_space=pl.ANY)
    received = pl.pallas_call(
        functools.partial(hand_over, pool_size, tp_size, most),
        out_shape=jax.ShapeDtypeStruct((slot_rows, local_heads * width), jnp.bfloat16),
        in_specs=[hbm, hbm, vmem, vmem, vmem],
        out_specs=vmem,
        scratch_shapes=[
            pltpu.VMEM(tokens.shape, jnp.bfloat16),
            pltpu.VMEM(w_kv.shape, jnp.bfloat16),
            pltpu.VMEM((heads, features, width), jnp.bfloat16),
            pltpu.VMEM((heads, rows, width), jnp.float32),
            pltpu.VMEM((chunks, chips, rows, LANES), jnp.float32),
            pltpu.VMEM((chunks, chips - 1, rows, LANES), jnp.float32),
            pltpu.VMEM((chunks, chips - 1, rows, LANES), jnp.float32),
            pltpu.VMEM((chunks, slot_rows, LANES), jnp.bfloat16),
            pltpu.VMEM((slot_rows, rows), jnp.bfloat16),
            pltpu.VMEM((rows, LANES), jnp.float32),
            pltpu.VMEM((rows, LANES), jnp.float32),
            pltpu.SemaphoreType.DMA((steps + 1,)),
            pltpu.SemaphoreType.DMA((2, chunks, chips)),
            pltpu.SemaphoreType.DMA((2, chunks, chips - 1)),
            pltpu.SemaphoreType.DMA((2, chunks, pool_size - 1)),
            pltpu.SemaphoreType.DMA((chunks,)),
        ],
        compiler_params=pltpu.CompilerParams(
            collective_id=0, has_side_effects=True, vmem_limit_bytes=56 * 2**20
        ),
    )(
        tokens,
        w_kv,
        jnp.concatenate([freqs, freqs])[None, :],
        prompt_lens[None, :],
        routes.reshape(1, -1),
    )
    return received.reshape(1, pool_size, most, BLOCK, local_heads, width)


def solution(mesh):
    placed = (P(("groups", "pool"), "tp"), P("tp", None, None), P("groups"), P("groups", None))
    return jax.shard_map(
        functools.partial(on_device, mesh.shape["pool"], mesh.shape["tp"]),
        mesh=mesh,
        in_specs=placed,
        out_specs=P(("groups", "pool"), None, None, None, "tp", None),
        check_vma=False,
    )
```

```python
import functools
import math

import jax
import jax.numpy as jnp
from jax import lax
from jax.experimental import pallas as pl
from jax.experimental.pallas import tpu as pltpu
from jax.sharding import PartitionSpec as P

BLOCK = 8
LANES = 128
DEPTH = 256
EARLY = 4
MESH = pl.DeviceIdType.MESH


def frequencies(head_dim):
    half = head_dim // 2
    base = jnp.exp(
        jnp.arange(half, dtype=jnp.float32) * (-2.0 / head_dim) * jnp.log(jnp.float32(500000.0))
    )
    wavelength = 2.0 * math.pi / base
    smooth = (8192.0 / wavelength - 1.0) / 3.0
    middle = (1.0 - smooth) * base / 8.0 + smooth * base
    return jnp.where(wavelength < 2048.0, base, jnp.where(wavelength > 8192.0, base / 8.0, middle))


def hand_over(
    pool_size, tp_size, most,
    tokens_hbm, w_hbm, freq_ref, lens_ref, route_ref,
    out_ref,
    tokens, w_in, w_heads, partial,
    pair_in, across_out, across_in, placed, select, cosine, sine,
    in_sems, pair_sems, across_sems, pool_sems, local_sems,
):
    pool_index = lax.axis_index("pool")
    tp_index = lax.axis_index("tp")
    chip, core = tp_index // 2, tp_index % 2
    chips = tp_size // 2
    rows = tokens.shape[0]
    local_heads = partial.shape[0] // tp_size
    parts = partial.shape[2] // LANES
    chunks = [(j, part) for j in range(local_heads) for part in range(parts)]
    span = most * BLOCK
    page_count = rows // BLOCK
    slot_rows = pool_size * span

    tokens_in = pltpu.make_async_copy(tokens_hbm, tokens, in_sems.at[0])
    depth = min(DEPTH, w_in.shape[0])
    steps = w_in.shape[0] // depth
    w_copies = [
        pltpu.make_async_copy(
            w_hbm.at[pl.ds(i * depth, depth)], w_in.at[pl.ds(i * depth, depth)], in_sems.at[i + 1]
        )
        for i in range(steps)
    ]
    tokens_in.start()
    for copy in w_copies:
        copy.start()

    def head_of(chip_of, core_of, j):
        return (chip_of * 2 + core_of) * local_heads + j

    barrier = pltpu.get_barrier_semaphore()
    peers = [{"tp": chip * 2 + 1 - core}]
    peers += [{"tp": lax.rem(chip + d, chips) * 2 + core} for d in range(1, chips)]
    peers += [{"pool": lax.rem(pool_index + d, pool_size)} for d in range(1, pool_size)]
    for peer in peers:
        pl.semaphore_signal(barrier, inc=1, device_id=peer, device_id_type=MESH)

    def head_for(d, core_of, j):
        return head_of(lax.rem(chip + d, chips), core_of, j)

    early = [
        head_for(d, side, j)
        for j in range(local_heads)
        for d in range(1, chips)
        for side in (1 - core, core)
    ][:EARLY]
    tokens_in.wait()
    for i, copy in enumerate(w_copies):
        copy.wait()
        block = slice(i * depth, (i + 1) * depth)
        w_heads[:, block, :] = jnp.swapaxes(w_in[block], 0, 1)
        for head in early:
            product = jnp.dot(
                tokens[:, block], w_heads[head, block, :], preferred_element_type=jnp.float32
            )
            partial[head] = product if i == 0 else partial[head] + product

    def multiply(head):
        partial[head] = jnp.dot(tokens[...], w_heads[head], preferred_element_type=jnp.float32)

    def window(head, part):
        return partial.at[head, :, pl.ds(part * LANES, LANES)]

    def pair_copy(n, d):
        j, part = chunks[n]
        return pltpu.make_async_remote_copy(
            src_ref=window(head_of(lax.rem(chip + d, chips), 1 - core, j), part),
            dst_ref=pair_in.at[n, d],
            send_sem=pair_sems.at[0, n, d],
            recv_sem=pair_sems.at[1, n, d],
            device_id={"tp": chip * 2 + 1 - core},
            device_id_type=MESH,
        )

    def across_copy(n, d):
        return pltpu.make_async_remote_copy(
            src_ref=across_out.at[n, d - 1],
            dst_ref=across_in.at[n, d - 1],
            send_sem=across_sems.at[0, n, d - 1],
            recv_sem=across_sems.at[1, n, d - 1],
            device_id={"tp": lax.rem(chip + d, chips) * 2 + core},
            device_id_type=MESH,
        )

    def pool_copy(n, d):
        target = lax.rem(pool_index + d, pool_size)
        return pltpu.make_async_remote_copy(
            src_ref=placed.at[n, pl.ds(pl.multiple_of(target * span, span), span)],
            dst_ref=out_ref.at[
                pl.ds(pl.multiple_of(pool_index * span, span), span), pl.ds(n * LANES, LANES)
            ],
            send_sem=pool_sems.at[0, n, d - 1],
            recv_sem=pool_sems.at[1, n, d - 1],
            device_id={"pool": target},
            device_id_type=MESH,
        )

    def own_copy(n):
        block = pl.ds(pl.multiple_of(pool_index * span, span), span)
        return pltpu.make_async_copy(
            placed.at[n, block], out_ref.at[block, pl.ds(n * LANES, LANES)], local_sems.at[n]
        )

    def to_pair(j, d, ready):
        if not ready:
            multiply(head_for(d, 1 - core, j))
        for part in range(parts):
            pair_copy(j * parts + part, d).start()

    def to_others(j, d):
        for part in range(parts):
            n = j * parts + part
            pair_copy(n, d).wait_recv()
            head = head_of(lax.rem(chip + d, chips), core, j)
            across_out[n, d - 1] = (
                partial[head, :, part * LANES:(part + 1) * LANES] + pair_in[n, d]
            )
            across_copy(n, d).start()

    pl.semaphore_wait(barrier, len(peers))
    others = [(j, d) for j in range(local_heads) for d in range(1, chips)]
    done = len(early) // 2
    for k, (j, d) in enumerate(others):
        to_pair(j, d, k < done)
    to_pair(0, 0, False)
    for k, (j, d) in enumerate(others):
        if k >= done:
            multiply(head_for(d, core, j))
        to_others(j, d)
    for j in range(1, local_heads):
        to_pair(j, 0, False)
    for j in range(local_heads):
        multiply(head_of(chip, core, j))

    def iota(shape, axis):
        return lax.broadcasted_iota(jnp.int32, shape, axis)

    def turned_row(column):
        count = column.shape[0]
        same = iota((count, count), 0) == iota((count, count), 1)
        return jnp.sum(jnp.where(same, column, 0.0), axis=0, keepdims=True)

    prompts = lens_ref.shape[1]
    lens = lens_ref[...].astype(jnp.float32)
    upto = iota((prompts, prompts), 1) <= iota((prompts, prompts), 0)
    ends = turned_row(jnp.sum(jnp.where(upto, lens, 0.0), axis=1, keepdims=True))
    token = (pool_index * rows + iota((rows, prompts), 0)).astype(jnp.float32)
    before = jnp.sum(jnp.where(ends <= token, lens, 0.0), axis=1, keepdims=True)
    position = token[:, :1] - before
    angle = position * freq_ref[...]
    cosine[...] = jnp.cos(angle)
    turned = jnp.sin(angle)
    sine[...] = jnp.where(iota((rows, LANES), 1) < LANES // 2, -turned, turned)

    pages = route_ref.shape[1]
    own_page = pool_index * page_count + (iota((rows, pages), 0) >> 3)
    target_col = jnp.sum(
        jnp.where(iota((rows, pages), 1) == own_page, route_ref[...].astype(jnp.float32), 0.0),
        axis=1,
        keepdims=True,
    )
    target_row = turned_row(target_col)
    earlier = (iota((rows, rows), 0) >> 3) < (iota((rows, rows), 1) >> 3)
    rank = jnp.sum(
        jnp.where(earlier & (target_col == target_row), 1.0, 0.0), axis=0, keepdims=True
    )
    slot = target_row * span + rank + (iota((1, rows), 1) & 7).astype(jnp.float32)
    select[...] = jnp.where(
        iota((slot_rows, rows), 0).astype(jnp.float32) == slot, 1.0, 0.0
    ).astype(jnp.bfloat16)

    for n, (j, part) in enumerate(chunks):
        pair_copy(n, 0).wait_recv()
        total = partial[head_of(chip, core, j), :, part * LANES:(part + 1) * LANES] + pair_in[n, 0]
        for d in range(1, chips):
            across_copy(n, d).wait_recv()
            total = total + across_in[n, d - 1]
        if part == 0:
            half = LANES // 2
            swapped = jnp.concatenate([total[:, half:], total[:, :half]], axis=1)
            total = total * cosine[...] + swapped * sine[...]
        placed[n] = jnp.dot(
            select[...], total.astype(jnp.bfloat16), preferred_element_type=jnp.float32
        ).astype(jnp.bfloat16)
        for d in range(1, pool_size):
            pool_copy(n, d).start()
        own_copy(n).start()

    for n in range(len(chunks)):
        own_copy(n).wait()
        for d in range(chips):
            pair_copy(n, d).wait_send()
        for d in range(1, chips):
            across_copy(n, d).wait_send()
        for d in range(1, pool_size):
            pool_copy(n, d).wait()


def on_device(pool_size, tp_size, tokens, w_kv, prompt_lens, routes):
    rows = tokens.shape[0]
    features, heads, width = w_kv.shape
    local_heads = heads // tp_size
    most = max(2, 2 * (rows // BLOCK) // pool_size)
    slot_rows = pool_size * most * BLOCK
    freqs = frequencies(width // 2)
    chunks = local_heads * width // LANES
    chips = tp_size // 2
    steps = max(1, features // DEPTH)
    vmem = pl.BlockSpec(memory_space=pltpu.VMEM)
    hbm = pl.BlockSpec(memory_space=pltpu.HBM)
    received = pl.pallas_call(
        functools.partial(hand_over, pool_size, tp_size, most),
        out_shape=jax.ShapeDtypeStruct((slot_rows, local_heads * width), jnp.bfloat16),
        in_specs=[hbm, hbm, vmem, vmem, vmem],
        out_specs=vmem,
        scratch_shapes=[
            pltpu.VMEM(tokens.shape, jnp.bfloat16),
            pltpu.VMEM(w_kv.shape, jnp.bfloat16),
            pltpu.VMEM((heads, features, width), jnp.bfloat16),
            pltpu.VMEM((heads, rows, width), jnp.float32),
            pltpu.VMEM((chunks, chips, rows, LANES), jnp.float32),
            pltpu.VMEM((chunks, chips - 1, rows, LANES), jnp.float32),
            pltpu.VMEM((chunks, chips - 1, rows, LANES), jnp.float32),
            pltpu.VMEM((chunks, slot_rows, LANES), jnp.bfloat16),
            pltpu.VMEM((slot_rows, rows), jnp.bfloat16),
            pltpu.VMEM((rows, LANES), jnp.float32),
            pltpu.VMEM((rows, LANES), jnp.float32),
            pltpu.SemaphoreType.DMA((steps + 1,)),
            pltpu.SemaphoreType.DMA((2, chunks, chips)),
            pltpu.SemaphoreType.DMA((2, chunks, chips - 1)),
            pltpu.SemaphoreType.DMA((2, chunks, pool_size - 1)),
            pltpu.SemaphoreType.DMA((chunks,)),
        ],
        compiler_params=pltpu.CompilerParams(
            collective_id=0, has_side_effects=True, vmem_limit_bytes=53 * 2**20
        ),
    )(
        tokens,
        w_kv,
        jnp.concatenate([freqs, freqs])[None, :],
        prompt_lens[None, :],
        routes.reshape(1, -1),
    )
    return received.reshape(1, pool_size, most, BLOCK, local_heads, width)


def solution(mesh):
    placed = (P(("groups", "pool"), "tp"), P("tp", None, None), P("groups"), P("groups", None))
    return jax.shard_map(
        functools.partial(on_device, mesh.shape["pool"], mesh.shape["tp"]),
        mesh=mesh,
        in_specs=placed,
        out_specs=P(("groups", "pool"), None, None, None, "tp", None),
        check_vma=False,
    )
```

```python
import functools
import math

import jax
import jax.numpy as jnp
from jax import lax
from jax.experimental import pallas as pl
from jax.experimental.pallas import tpu as pltpu
from jax.sharding import PartitionSpec as P

BLOCK = 8
LANES = 128
DEPTH = 256
EARLY = 4
MESH = pl.DeviceIdType.MESH


def frequencies(head_dim):
    half = head_dim // 2
    base = jnp.exp(
        jnp.arange(half, dtype=jnp.float32) * (-2.0 / head_dim) * jnp.log(jnp.float32(500000.0))
    )
    wavelength = 2.0 * math.pi / base
    smooth = (8192.0 / wavelength - 1.0) / 3.0
    middle = (1.0 - smooth) * base / 8.0 + smooth * base
    return jnp.where(wavelength < 2048.0, base, jnp.where(wavelength > 8192.0, base / 8.0, middle))


def hand_over(
    pool_size, tp_size, most,
    tokens_hbm, w_hbm, freq_ref, lens_ref, route_ref,
    out_ref,
    tokens, w_in, w_heads, partial,
    pair_in, across_out, across_in, placed, select, cosine, sine,
    in_sems, pair_sems, across_sems, pool_sems, local_sems,
):
    pool_index = lax.axis_index("pool")
    tp_index = lax.axis_index("tp")
    chip, core = tp_index // 2, tp_index % 2
    chips = tp_size // 2
    rows = tokens.shape[0]
    local_heads = partial.shape[0] // tp_size
    parts = partial.shape[2] // LANES
    chunks = [(j, part) for j in range(local_heads) for part in range(parts)]
    span = most * BLOCK
    page_count = rows // BLOCK
    slot_rows = pool_size * span

    tokens_in = pltpu.make_async_copy(tokens_hbm, tokens, in_sems.at[0])
    depth = min(DEPTH, w_in.shape[0])
    steps = w_in.shape[0] // depth
    w_copies = [
        pltpu.make_async_copy(
            w_hbm.at[pl.ds(i * depth, depth)], w_in.at[pl.ds(i * depth, depth)], in_sems.at[i + 1]
        )
        for i in range(steps)
    ]
    tokens_in.start()
    for copy in w_copies:
        copy.start()

    def head_of(chip_of, core_of, j):
        return (chip_of * 2 + core_of) * local_heads + j

    barrier = pltpu.get_barrier_semaphore()
    peers = [{"tp": chip * 2 + 1 - core}]
    peers += [{"tp": lax.rem(chip + d, chips) * 2 + core} for d in range(1, chips)]
    peers += [{"pool": lax.rem(pool_index + d, pool_size)} for d in range(1, pool_size)]
    for peer in peers:
        pl.semaphore_signal(barrier, inc=1, device_id=peer, device_id_type=MESH)

    def head_for(d, core_of, j):
        return head_of(lax.rem(chip + d, chips), core_of, j)

    early = [
        head_for(d, side, j)
        for j in range(local_heads)
        for d in range(1, chips)
        for side in (1 - core, core)
    ][:EARLY]
    tokens_in.wait()
    for i, copy in enumerate(w_copies):
        copy.wait()
        block = slice(i * depth, (i + 1) * depth)
        w_heads[:, block, :] = jnp.swapaxes(w_in[block], 0, 1)
        for head in early:
            product = jnp.dot(
                tokens[:, block], w_heads[head, block, :], preferred_element_type=jnp.float32
            )
            partial[head] = product if i == 0 else partial[head] + product

    def multiply(head):
        partial[head] = jnp.dot(tokens[...], w_heads[head], preferred_element_type=jnp.float32)

    def window(head, part):
        return partial.at[head, :, pl.ds(part * LANES, LANES)]

    def pair_copy(n, d):
        j, part = chunks[n]
        return pltpu.make_async_remote_copy(
            src_ref=window(head_of(lax.rem(chip + d, chips), 1 - core, j), part),
            dst_ref=pair_in.at[n, d],
            send_sem=pair_sems.at[0, n, d],
            recv_sem=pair_sems.at[1, n, d],
            device_id={"tp": chip * 2 + 1 - core},
            device_id_type=MESH,
        )

    def across_copy(n, d):
        return pltpu.make_async_remote_copy(
            src_ref=across_out.at[n, d - 1],
            dst_ref=across_in.at[n, d - 1],
            send_sem=across_sems.at[0, n, d - 1],
            recv_sem=across_sems.at[1, n, d - 1],
            device_id={"tp": lax.rem(chip + d, chips) * 2 + core},
            device_id_type=MESH,
        )

    def pool_copy(n, d):
        target = lax.rem(pool_index + d, pool_size)
        return pltpu.make_async_remote_copy(
            src_ref=placed.at[n, pl.ds(pl.multiple_of(target * span, span), span)],
            dst_ref=out_ref.at[
                pl.ds(pl.multiple_of(pool_index * span, span), span), pl.ds(n * LANES, LANES)
            ],
            send_sem=pool_sems.at[0, n, d - 1],
            recv_sem=pool_sems.at[1, n, d - 1],
            device_id={"pool": target},
            device_id_type=MESH,
        )

    def own_copy(n):
        block = pl.ds(pl.multiple_of(pool_index * span, span), span)
        return pltpu.make_async_copy(
            placed.at[n, block], out_ref.at[block, pl.ds(n * LANES, LANES)], local_sems.at[n]
        )

    def to_pair(j, d, ready):
        if not ready:
            multiply(head_for(d, 1 - core, j))
        for part in range(parts):
            pair_copy(j * parts + part, d).start()

    def to_others(j, d):
        for part in range(parts):
            n = j * parts + part
            pair_copy(n, d).wait_recv()
            head = head_of(lax.rem(chip + d, chips), core, j)
            across_out[n, d - 1] = (
                partial[head, :, part * LANES:(part + 1) * LANES] + pair_in[n, d]
            )
            if n == 0:
                across_copy(n, d).start()

    pl.semaphore_wait(barrier, len(peers))
    others = [(j, d) for j in range(local_heads) for d in range(1, chips)]
    done = len(early) // 2
    for k, (j, d) in enumerate(others):
        to_pair(j, d, k < done)
    to_pair(0, 0, False)
    for k, (j, d) in enumerate(others):
        if k >= done:
            multiply(head_for(d, core, j))
        to_others(j, d)
    for j in range(1, local_heads):
        to_pair(j, 0, False)
    for j in range(local_heads):
        multiply(head_of(chip, core, j))
    for n in range(1, min(2, len(chunks))):
        for d in range(1, chips):
            across_copy(n, d).start()

    def iota(shape, axis):
        return lax.broadcasted_iota(jnp.int32, shape, axis)

    def turned_row(column):
        count = column.shape[0]
        same = iota((count, count), 0) == iota((count, count), 1)
        return jnp.sum(jnp.where(same, column, 0.0), axis=0, keepdims=True)

    prompts = lens_ref.shape[1]
    lens = lens_ref[...].astype(jnp.float32)
    upto = iota((prompts, prompts), 1) <= iota((prompts, prompts), 0)
    ends = turned_row(jnp.sum(jnp.where(upto, lens, 0.0), axis=1, keepdims=True))
    token = (pool_index * rows + iota((rows, prompts), 0)).astype(jnp.float32)
    before = jnp.sum(jnp.where(ends <= token, lens, 0.0), axis=1, keepdims=True)
    position = token[:, :1] - before
    angle = position * freq_ref[...]
    cosine[...] = jnp.cos(angle)
    turned = jnp.sin(angle)
    sine[...] = jnp.where(iota((rows, LANES), 1) < LANES // 2, -turned, turned)

    pages = route_ref.shape[1]
    own_page = pool_index * page_count + (iota((rows, pages), 0) >> 3)
    target_col = jnp.sum(
        jnp.where(iota((rows, pages), 1) == own_page, route_ref[...].astype(jnp.float32), 0.0),
        axis=1,
        keepdims=True,
    )
    target_row = turned_row(target_col)
    earlier = (iota((rows, rows), 0) >> 3) < (iota((rows, rows), 1) >> 3)
    rank = jnp.sum(
        jnp.where(earlier & (target_col == target_row), 1.0, 0.0), axis=0, keepdims=True
    )
    slot = target_row * span + rank + (iota((1, rows), 1) & 7).astype(jnp.float32)
    select[...] = jnp.where(
        iota((slot_rows, rows), 0).astype(jnp.float32) == slot, 1.0, 0.0
    ).astype(jnp.bfloat16)

    for n, (j, part) in enumerate(chunks):
        pair_copy(n, 0).wait_recv()
        total = partial[head_of(chip, core, j), :, part * LANES:(part + 1) * LANES] + pair_in[n, 0]
        for d in range(1, chips):
            across_copy(n, d).wait_recv()
            total = total + across_in[n, d - 1]
            if n + 2 < len(chunks):
                across_copy(n + 2, d).start()
        if part == 0:
            half = LANES // 2
            swapped = jnp.concatenate([total[:, half:], total[:, :half]], axis=1)
            total = total * cosine[...] + swapped * sine[...]
        placed[n] = jnp.dot(
            select[...], total.astype(jnp.bfloat16), preferred_element_type=jnp.float32
        ).astype(jnp.bfloat16)
        for d in range(1, pool_size):
            pool_copy(n, d).start()
        own_copy(n).start()

    for n in range(len(chunks)):
        own_copy(n).wait()
        for d in range(chips):
            pair_copy(n, d).wait_send()
        for d in range(1, chips):
            across_copy(n, d).wait_send()
        for d in range(1, pool_size):
            pool_copy(n, d).wait()


def on_device(pool_size, tp_size, tokens, w_kv, prompt_lens, routes):
    rows = tokens.shape[0]
    features, heads, width = w_kv.shape
    local_heads = heads // tp_size
    most = max(2, 2 * (rows // BLOCK) // pool_size)
    slot_rows = pool_size * most * BLOCK
    freqs = frequencies(width // 2)
    chunks = local_heads * width // LANES
    chips = tp_size // 2
    steps = max(1, features // DEPTH)
    vmem = pl.BlockSpec(memory_space=pltpu.VMEM)
    hbm = pl.BlockSpec(memory_space=pltpu.HBM)
    received = pl.pallas_call(
        functools.partial(hand_over, pool_size, tp_size, most),
        out_shape=jax.ShapeDtypeStruct((slot_rows, local_heads * width), jnp.bfloat16),
        in_specs=[hbm, hbm, vmem, vmem, vmem],
        out_specs=vmem,
        scratch_shapes=[
            pltpu.VMEM(tokens.shape, jnp.bfloat16),
            pltpu.VMEM(w_kv.shape, jnp.bfloat16),
            pltpu.VMEM((heads, features, width), jnp.bfloat16),
            pltpu.VMEM((heads, rows, width), jnp.float32),
            pltpu.VMEM((chunks, chips, rows, LANES), jnp.float32),
            pltpu.VMEM((chunks, chips - 1, rows, LANES), jnp.float32),
            pltpu.VMEM((chunks, chips - 1, rows, LANES), jnp.float32),
            pltpu.VMEM((chunks, slot_rows, LANES), jnp.bfloat16),
            pltpu.VMEM((slot_rows, rows), jnp.bfloat16),
            pltpu.VMEM((rows, LANES), jnp.float32),
            pltpu.VMEM((rows, LANES), jnp.float32),
            pltpu.SemaphoreType.DMA((steps + 1,)),
            pltpu.SemaphoreType.DMA((2, chunks, chips)),
            pltpu.SemaphoreType.DMA((2, chunks, chips - 1)),
            pltpu.SemaphoreType.DMA((2, chunks, pool_size - 1)),
            pltpu.SemaphoreType.DMA((chunks,)),
        ],
        compiler_params=pltpu.CompilerParams(
            collective_id=0, has_side_effects=True, vmem_limit_bytes=53 * 2**20
        ),
    )(
        tokens,
        w_kv,
        jnp.concatenate([freqs, freqs])[None, :],
        prompt_lens[None, :],
        routes.reshape(1, -1),
    )
    return received.reshape(1, pool_size, most, BLOCK, local_heads, width)


def solution(mesh):
    placed = (P(("groups", "pool"), "tp"), P("tp", None, None), P("groups"), P("groups", None))
    return jax.shard_map(
        functools.partial(on_device, mesh.shape["pool"], mesh.shape["tp"]),
        mesh=mesh,
        in_specs=placed,
        out_specs=P(("groups", "pool"), None, None, None, "tp", None),
        check_vma=False,
    )
```
